32 devices in a mesh: group: 2 (over y), term: 4 (over x, core), sector: 4 (over z).
Axes of the slice: x: 2, y: 2, z: 4, core: 2. Of those that a mesh axis runs over, the one named last changes fastest.
Arguments:
- trial: float32 [8, 256, 256], P(('group', 'sector'), 'term'), parts along dimension 0, may hold values from -6 to 6
- precond: float32 [8, 256, 256], P(('group', 'sector'), 'term'), parts along dimension 0, may hold values from 1 to 8
- left_ops: float32 [48, 4, 256, 256], P(('group', 'term'), 'sector'), parts along dimension 0, may hold values from -0.375 to 0.375
- right_ops: float32 [48, 4, 256, 256], P(('group', 'term'), 'sector'), parts along dimension 0, may hold values from -0.375 to 0.375
- links: int32 [48, 4], P(('group', 'term'), 'sector'), parts along dimension 0, may hold values from 0 to 4, as said below
- block_dims: int32 [8, 2], P(('group', 'sector')), parts along dimension 0, may hold values from 128 to 256, as said below
Outputs:
- ground: float32 [8, 256, 256], P(('group', 'sector'), 'term'), parts along dimension 0
- energy: float32 [2], P('group'), parts along dimension 0
The draws below stay inside these ranges and needn't reach their ends.
There are 2 independent parts, one for each index of `group`. The reference program is written for one: setup_inputs(seed, part) draws one part's arguments, and reference() takes and returns one part's arrays. A program takes and returns all parts, laid end to end along the dimension named above; each array names one. Nothing has to cross between parts.
Inputs may be any that keep to these rules, and one draw needn't show every extreme that they name: `links`: 4 marks a term that has no block for that target. `block_dims`: entries beyond these are padding.
All inputs are finite; a program needn't handle non-finite values.
Results may differ from the reference program's by a relative error of at most 0.0003.
Values sent between devices are 32-bit elements; how exact they have to be, the bound alone decides.
A program may use at most 64 MiB of HBM per device.

```python
import math
import jax
import jax.numpy as jnp
from jax import lax

BLK = 256
ITERS = 3
NBLK = 4
TERMS = 24


def draw_links(key, part):
    key = jax.random.fold_in(key, 11)
    first, second = jax.random.split(key)
    shifts = jax.random.randint(first, (TERMS, 1), 0, NBLK)
    target = jnp.arange(NBLK)[None, :]
    source = (target - shifts) % NBLK
    absent = jax.random.randint(second, (TERMS, NBLK), 0, 4) == 0
    forced = target == jnp.arange(TERMS)[:, None] % NBLK
    return jnp.where(absent | forced, NBLK, source).astype(jnp.int32)


def draw_block_dims(key, part):
    key = jax.random.fold_in(key, 12)
    dims = jax.random.randint(key, (NBLK, 2), BLK // 2, BLK + 1)
    dims = dims.at[0].set(BLK)
    dims = dims.at[1].set(BLK // 2)
    return dims.astype(jnp.int32)


def level_of(rng, shape, shards, smallest, largest):
    level, own = 1.0, jax.random.fold_in(rng, 6)
    for axis_at, blocks in shards:
        steps = jnp.exp(jax.random.uniform(jax.random.fold_in(own, axis_at), (blocks,), jnp.float32, smallest / len(shards), largest / len(shards)))
        level = level * jnp.repeat(steps, shape[axis_at] // blocks).reshape([-1 if axis == axis_at else 1 for axis in range(len(shape))])
    return level


def normal_values(stream_key, extent, scale, bound, pieces=(), kind=jnp.bfloat16):
    entries = scale * jax.random.normal(stream_key, extent, jnp.float32)
    if pieces:
        entries = entries * level_of(stream_key, extent, pieces, -0.22, 0.18)
    return jnp.clip(entries, -bound, bound).astype(kind)


def setup_inputs(seed: int = 0, part: int = 0) -> dict:
    keys = jax.random.split(jax.random.key(seed), 7)
    part_keys = jax.random.split(jax.random.fold_in(keys[6], part), 7)
    return {
        "trial": normal_values(part_keys[0], (NBLK, BLK, BLK), 1.0, 6.0, ((0, 4), (1, 4)), jnp.float32),
        "precond": jnp.clip(jnp.exp(math.log(8.0) - 2.0794415 * jax.random.uniform(part_keys[1], (NBLK, BLK, BLK), jnp.float32) ** level_of(part_keys[1], (NBLK, BLK, BLK), ((0, 4), (1, 4)), -0.2, 0.2)), 1.0, 8.0),
        "left_ops": normal_values(part_keys[2], (TERMS, NBLK, BLK, BLK), BLK ** -0.5, 0.375, ((0, 4), (1, 4)), jnp.float32),
        "right_ops": normal_values(part_keys[3], (TERMS, NBLK, BLK, BLK), BLK ** -0.5, 0.375, ((0, 4), (1, 4)), jnp.float32),
        "links": draw_links(jax.random.fold_in(jax.random.fold_in(keys[6], part), 71), part),
        "block_dims": draw_block_dims(jax.random.fold_in(jax.random.fold_in(keys[6], part), 71), part),
    }


EPS = 1e-06

def block_mask(block_dims):
    index = jnp.arange(BLK)
    rows = index[None, :, None] < block_dims[:, 0][:, None, None]
    cols = index[None, None, :] < block_dims[:, 1][:, None, None]
    return (rows & cols).astype(jnp.float32)

def apply_op(vector, left_ops, right_ops, links, mask):
    padded = jnp.concatenate([vector, jnp.zeros((1, BLK, BLK), jnp.float32)], 0)

    def step(total, item):
        left, right, link = item
        chosen = jnp.take(padded, link.astype(jnp.int32), axis=0)
        inner = jnp.einsum('kab,kbc->kac', left, chosen, precision=lax.Precision.HIGHEST)
        return (total + jnp.einsum('kac,kdc->kad', inner, right, precision=lax.Precision.HIGHEST), None)
    total, unused = lax.scan(step, jnp.zeros((NBLK, BLK, BLK), jnp.float32), (left_ops, right_ops, links))
    return total * mask

def reference(trial, precond, left_ops, right_ops, links, block_dims):
    count = float(NBLK * BLK * BLK)
    mask = block_mask(block_dims)

    def inner(first, second):
        return jnp.sum(first * second) / count
    vector = trial * mask
    vector = vector / jnp.sqrt(inner(vector, vector) + EPS)
    image = apply_op(vector, left_ops, right_ops, links, mask)
    theta = inner(vector, image)
    for step in range(ITERS):
        resid = image - theta * vector
        raw = resid / precond
        proj = raw - inner(vector, raw) * vector
        basis = proj / jnp.sqrt(inner(proj, proj) + EPS)
        himage = apply_op(basis, left_ops, right_ops, links, mask)
        diag_a = theta
        cross = 0.5 * (inner(vector, himage) + inner(basis, image))
        diag_c = inner(basis, himage)
        half = 0.5 * (diag_a - diag_c)
        spread = jnp.sqrt(half * half + cross * cross)
        lowest = 0.5 * (diag_a + diag_c) - spread
        coef_x = spread - half
        coef_y = -cross
        length = jnp.sqrt(coef_x * coef_x + coef_y * coef_y)
        vector = (coef_x * vector + coef_y * basis) / length
        image = (coef_x * image + coef_y * himage) / length
        theta = lowest
    return (vector, jnp.reshape(theta, (1,)))
```

```python
import functools

import jax
import jax.numpy as jnp
from jax import lax
from jax.experimental import pallas as pl
from jax.experimental.pallas import tpu as pltpu
from jax.sharding import PartitionSpec as P

ITERS = 3
EPS = 1e-06
CORES = 2
CHUNK = 64
MESH = pl.DeviceIdType.MESH
F32 = jnp.float32
BF16 = jnp.bfloat16


def split(value):
    high = value.astype(BF16)
    low = (value - high.astype(F32)).astype(BF16)
    return high, low


def kernel(
    sectors, terms, count,
    links_ref, dims_ref, trial_ref, pre_ref, left_ref, right_ref,
    ground_ref, energy_ref,
    gath, part, rsbuf, vec, img, res, pinv, xcat, lcat, rcat, icat, lraw, rraw,
    ag_send, ag_recv, rs_send, rs_recv, load_sem,
):
    rows, width = trial_ref.shape
    own_terms = lraw.shape[0]
    chips = terms // CORES
    me_t = lax.axis_index("term")
    me_s = lax.axis_index("sector")
    me_x = me_t // CORES
    me_c = lax.rem(me_t, CORES)
    other_c = (CORES - 1) - me_c
    wide = 3 * width
    total_rows = sectors * width
    steps = total_rows // CHUNK
    per_block = width // CHUNK

    def term_at(x, c):
        return x * CORES + c

    def ring(i, d, n):
        return lax.rem(i + d + n, n)

    loads = [
        pltpu.make_async_copy(left_ref, lraw, load_sem.at[0]),
        pltpu.make_async_copy(right_ref, rraw, load_sem.at[1]),
    ]
    for load in loads:
        load.start()

    barrier = pltpu.get_barrier_semaphore()
    for d in range(1, sectors):
        pl.semaphore_signal(
            barrier, inc=1, device_id={"sector": ring(me_s, d, sectors)}, device_id_type=MESH
        )
    for d in range(1, terms):
        pl.semaphore_signal(
            barrier, inc=1, device_id={"term": ring(me_t, d, terms)}, device_id_type=MESH
        )
    pl.semaphore_wait(barrier, sectors + terms - 2)

    def slab(ag, s, t):
        return gath.at[ag, pl.ds(pl.multiple_of(s * width + t * rows, rows), rows)]

    def slab_copy(ag, s, t, to_s, to_t, k):
        here = slab(ag, s, t)
        return pltpu.make_async_remote_copy(
            src_ref=here, dst_ref=here,
            send_sem=ag_send.at[ag, k], recv_sem=ag_recv.at[ag, s * terms + t],
            device_id={"term": to_t, "sector": to_s}, device_id_type=MESH,
        )

    def arrive(ag, s, t):
        slab_copy(ag, s, t, ring(me_s, 1, sectors), me_t, 0).wait_recv()

    k_x = sectors - 1
    k_c = k_x + (chips - 1) * sectors
    n_send = k_c + chips * sectors

    def to_chips(ag, s, d):
        for e in range(1, chips):
            slab_copy(
                ag, s, me_t, me_s, term_at(ring(me_x, e, chips), me_c),
                k_x + (e - 1) * sectors + d,
            ).start()

    def to_core(ag, s, x, d, e):
        slab_copy(
            ag, s, term_at(x, me_c), me_s, term_at(me_x, other_c), k_c + e * sectors + d
        ).start()

    def gather_start(ag):
        for d in range(1, sectors):
            slab_copy(ag, me_s, me_t, ring(me_s, d, sectors), me_t, d - 1).start()
        to_chips(ag, me_s, 0)
        to_core(ag, me_s, me_x, 0, 0)

    def gather_sector(ag):
        for d in range(1, sectors):
            s = ring(me_s, -d, sectors)
            arrive(ag, s, me_t)
            to_chips(ag, s, d)
            to_core(ag, s, me_x, d, 0)

    def gather_chip(ag):
        for e in range(1, chips):
            x = ring(me_x, -e, chips)
            for d in range(sectors):
                s = ring(me_s, -d, sectors)
                arrive(ag, s, term_at(x, me_c))
                to_core(ag, s, x, d, e)

    def gather_core(ag):
        for e in range(chips):
            x = ring(me_x, -e, chips)
            for d in range(sectors):
                arrive(ag, ring(me_s, -d, sectors), term_at(x, other_c))

    def gather_rest(ag):
        gather_sector(ag)
        gather_chip(ag)
        gather_core(ag)

    def fold(value):
        return jnp.sum(value.reshape(CHUNK // 8, 8, width), axis=0)

    def chunk_of(i):
        return pl.ds(pl.multiple_of(i * CHUNK, CHUNK), CHUNK)

    def dots(pick, n):
        def body(i, sums):
            at = chunk_of(i)
            return tuple(a + fold(p) for a, p in zip(sums, pick(at)))

        zero = jnp.zeros((8, width), F32)
        sums = lax.fori_loop(0, steps, body, (zero,) * n, unroll=2)
        out = []
        for a in sums:
            a = jnp.sum(a, axis=0, keepdims=True)
            out.append(jnp.sum(a, axis=1, keepdims=True) / count)
        return out

    def put_x(i, value):
        high, low = split(value)
        block = i // per_block
        off = pl.multiple_of(lax.rem(i, per_block) * CHUNK, CHUNK)
        xcat[block, pl.ds(off, CHUNK), :] = high
        xcat[block, pl.ds(width + off, CHUNK), :] = low
        xcat[block, pl.ds(2 * width + off, CHUNK), :] = high

    def over_chunks(body):
        def step(i, carry):
            body(i, chunk_of(i))
            return carry

        lax.fori_loop(0, steps, step, 0, unroll=2)

    row_index = me_t * rows + lax.broadcasted_iota(jnp.int32, (rows, width), 0)
    col_index = lax.broadcasted_iota(jnp.int32, (rows, width), 1)
    live = (row_index < dims_ref[0]) & (col_index < dims_ref[1])
    mask = jnp.where(live, F32(1), F32(0))
    own = pl.ds(pl.multiple_of(me_s * width + me_t * rows, rows), rows)
    first, pre = ITERS + 1, ITERS + 2
    gath[first, own, :] = trial_ref[...] * mask
    gath[pre, own, :] = pre_ref[...]
    gather_start(first)
    for load in loads:
        load.wait()
    xcat[sectors] = jnp.zeros((wide, width), BF16)

    def prepare(k, carry):
        high, low = split(lraw[k])
        lcat[k, :, 0:width] = high
        lcat[k, :, width : 2 * width] = high
        lcat[k, :, 2 * width :] = low
        high, low = split(rraw[k].T)
        base = pl.multiple_of(k * wide, wide)
        rcat[pl.ds(base, width), :] = high
        rcat[pl.ds(base + width, width), :] = low
        rcat[pl.ds(base + 2 * width, width), :] = high
        return carry

    gather_sector(first)
    lax.fori_loop(0, own_terms, prepare, 0)
    gather_chip(first)
    gather_core(first)
    gather_start(pre)

    (norm,) = dots(lambda at: (gath[first, at, :] * gath[first, at, :],), 1)
    scale = 1.0 / jnp.sqrt(norm + EPS)

    def begin(i, at):
        value = gath[first, at, :] * scale
        vec[at, :] = value
        put_x(i, value)

    over_chunks(begin)

    def rs_copy(it, d):
        to = ring(me_t, d, terms)
        return pltpu.make_async_remote_copy(
            src_ref=part.at[it, pl.ds(pl.multiple_of(to * rows, rows), rows)],
            dst_ref=rsbuf.at[it, d - 1],
            send_sem=rs_send.at[it, d - 1], recv_sem=rs_recv.at[it, d - 1],
            device_id={"term": to}, device_id_type=MESH,
        )

    def multiply(it):
        for k in range(own_terms):
            inner = jnp.dot(lcat[k], xcat[links_ref[k]], preferred_element_type=F32)
            high, low = split(inner)
            icat[:, k * wide : k * wide + width] = high
            icat[:, k * wide + width : k * wide + 2 * width] = high
            icat[:, k * wide + 2 * width : (k + 1) * wide] = low
        part[it] = jnp.dot(icat[...], rcat[...], preferred_element_type=F32)
        for d in range(1, terms):
            rs_copy(it, d).start()

    def collect(it):
        total = part[it, pl.ds(pl.multiple_of(me_t * rows, rows), rows), :]
        for d in range(1, terms):
            rs_copy(it, d).wait_recv()
            total = total + rsbuf[it, d - 1]
        gath[it, own, :] = total * mask
        gather_start(it)

    multiply(0)
    gather_sector(pre)
    collect(0)
    gather_chip(pre)
    gather_core(pre)

    def invert(i, at):
        pinv[at, :] = 1.0 / gath[pre, at, :]

    over_chunks(invert)
    gather_rest(0)
    (theta,) = dots(lambda at: (vec[at, :] * gath[0, at, :],), 1)

    def begin_residual(i, at):
        w = gath[0, at, :]
        img[at, :] = w
        r = (w - theta * vec[at, :]) * pinv[at, :]
        res[at, :] = r
        put_x(i, r)

    over_chunks(begin_residual)

    def iterate(it, theta):
        multiply(it)

        def early(at):
            v, w, r = vec[at, :], img[at, :], res[at, :]
            return v * v, v * w, v * r, r * r, r * w

        vv, vw, along, rr, rw = dots(early, 5)
        collect(it)
        gather_rest(it)

        def late(at):
            h = gath[it, at, :]
            return vec[at, :] * h, res[at, :] * h

        vh, rh = dots(late, 2)
        proj = rr - 2.0 * along * along + along * along * vv
        g = 1.0 / jnp.sqrt(proj + EPS)
        cross = 0.5 * g * ((vh - along * vw) + (rw - along * vw))
        diag_c = g * g * (rh - along * (rw + vh) + along * along * vw)
        half = 0.5 * (theta - diag_c)
        spread = jnp.sqrt(half * half + cross * cross)
        lowest = 0.5 * (theta + diag_c) - spread
        coef_x = spread - half
        coef_y = -cross
        length = jnp.sqrt(coef_x * coef_x + coef_y * coef_y)
        c_new = coef_y * g / length
        c_old = (coef_x - coef_y * g * along) / length

        def update(i, at):
            v = c_old * vec[at, :] + c_new * res[at, :]
            w = c_old * img[at, :] + c_new * gath[it, at, :]
            vec[at, :] = v
            img[at, :] = w
            r = (w - lowest * v) * pinv[at, :]
            res[at, :] = r
            put_x(i, r)

        over_chunks(update)
        return lowest

    theta = lax.fori_loop(1, ITERS + 1, iterate, theta)
    ground_ref[...] = vec[own, :]
    energy_ref[...] = jnp.broadcast_to(theta, energy_ref.shape)

    def finish(ag, carry):
        for k in range(n_send):
            slab_copy(ag, me_s, me_t, ring(me_s, 1, sectors), me_t, k).wait_send()
        return carry

    lax.fori_loop(0, ITERS + 3, finish, 0)

    def finish_rs(it, carry):
        for d in range(1, terms):
            rs_copy(it, d).wait_send()
        return carry

    lax.fori_loop(0, ITERS + 1, finish_rs, 0)


def on_device(trial, precond, left_ops, right_ops, links, block_dims):
    sectors = lax.axis_size("sector")
    terms = lax.axis_size("term")
    _, rows, width = trial.shape
    own_terms = left_ops.shape[0]
    count = float(sectors * width * width)
    applies = ITERS + 1
    gathers = ITERS + 3
    whole = (sectors * width, width)
    vmem = pl.BlockSpec(memory_space=pltpu.VMEM)
    smem = pl.BlockSpec(memory_space=pltpu.SMEM)
    hbm = pl.BlockSpec(memory_space=pl.ANY)
    ground, energy = pl.pallas_call(
        functools.partial(kernel, sectors, terms, count),
        out_shape=(
            jax.ShapeDtypeStruct((rows, width), F32),
            jax.ShapeDtypeStruct((1, 128), F32),
        ),
        in_specs=[smem, smem, vmem, vmem, hbm, hbm],
        out_specs=(vmem, vmem),
        scratch_shapes=[
            pltpu.VMEM((gathers,) + whole, F32),
            pltpu.VMEM((applies, width, width), F32),
            pltpu.VMEM((applies, terms - 1, rows, width), F32),
            pltpu.VMEM(whole, F32),
            pltpu.VMEM(whole, F32),
            pltpu.VMEM(whole, F32),
            pltpu.VMEM(whole, F32),
            pltpu.VMEM((sectors + 1, 3 * width, width), BF16),
            pltpu.VMEM((own_terms, width, 3 * width), BF16),
            pltpu.VMEM((own_terms * 3 * width, width), BF16),
            pltpu.VMEM((width, own_terms * 3 * width), BF16),
            pltpu.VMEM((own_terms, width, width), F32),
            pltpu.VMEM((own_terms, width, width), F32),
            pltpu.SemaphoreType.DMA((gathers, sectors * terms)),
            pltpu.SemaphoreType.DMA((gathers, sectors * terms)),
            pltpu.SemaphoreType.DMA((applies, terms - 1)),
            pltpu.SemaphoreType.DMA((applies, terms - 1)),
            pltpu.SemaphoreType.DMA((2,)),
        ],
        compiler_params=pltpu.CompilerParams(
            collective_id=0, has_side_effects=True, vmem_limit_bytes=52 * 2**20
        ),
    )(
        links.reshape(own_terms),
        block_dims.reshape(2),
        trial.reshape(rows, width),
        precond.reshape(rows, width),
        left_ops.reshape(own_terms, width, width),
        right_ops.reshape(own_terms, width, width),
    )
    return ground.reshape(1, rows, width), energy[0, :1]


def solution(mesh):
    in_specs = (
        P(("group", "sector"), "term", None),
        P(("group", "sector"), "term", None),
        P(("group", "term"), "sector", None, None),
        P(("group", "term"), "sector", None, None),
        P(("group", "term"), "sector"),
        P(("group", "sector"), None),
    )
    out_specs = (P(("group", "sector"), "term", None), P("group"))
    return jax.shard_map(
        on_device, mesh=mesh, in_specs=in_specs, out_specs=out_specs, check_vma=False
    )
```

```python
import functools

import jax
import jax.numpy as jnp
from jax import lax
from jax.experimental import pallas as pl
from jax.experimental.pallas import tpu as pltpu
from jax.sharding import PartitionSpec as P

ITERS = 3
EPS = 1e-06
CORES = 2
CHUNK = 64
MESH = pl.DeviceIdType.MESH
F32 = jnp.float32
BF16 = jnp.bfloat16


def split(value):
    high = value.astype(BF16)
    low = (value - high.astype(F32)).astype(BF16)
    return high, low


def kernel(
    sectors, terms, count,
    links_ref, dims_ref, trial_ref, pre_ref, left_ref, right_ref,
    ground_ref, energy_ref,
    gath, part, rsbuf, vec, img, res, pinv, xcat, lcat, rcat, icat, lraw, rraw, traw, scal,
    ag_send, ag_recv, rs_send, rs_recv, sc_send, sc_recv, load_sem,
):
    rows, width = traw.shape
    own_terms = lraw.shape[0]
    chips = terms // CORES
    me_t = lax.axis_index("term")
    me_s = lax.axis_index("sector")
    me_x = me_t // CORES
    me_c = lax.rem(me_t, CORES)
    other_c = (CORES - 1) - me_c
    wide = 3 * width
    total_rows = sectors * width
    steps = total_rows // CHUNK
    per_block = width // CHUNK

    def term_at(x, c):
        return x * CORES + c

    def ring(i, d, n):
        return lax.rem(i + d + n, n)

    others = [(a, b) for a in range(sectors) for b in range(terms) if a or b]
    barrier = pltpu.get_barrier_semaphore()
    for a, b in others:
        pl.semaphore_signal(
            barrier, inc=1,
            device_id={"term": ring(me_t, b, terms), "sector": ring(me_s, a, sectors)},
            device_id_type=MESH,
        )
    first, pre = ITERS, ITERS + 1
    own = pl.ds(pl.multiple_of(me_s * width + me_t * rows, rows), rows)
    trial_load = pltpu.make_async_copy(trial_ref, traw, load_sem.at[2])
    pre_load = pltpu.make_async_copy(pre_ref, gath.at[pre, own], load_sem.at[3])
    loads = [
        pltpu.make_async_copy(left_ref, lraw, load_sem.at[0]),
        pltpu.make_async_copy(right_ref, rraw, load_sem.at[1]),
    ]
    trial_load.start()
    for load in loads:
        load.start()
    pre_load.start()

    if sectors == 4:
        to_sector = [
            me_s + 1 - 2 * lax.rem(me_s, 2),
            lax.rem(me_s + 2, 4),
            3 - me_s,
        ]
        from_sector = to_sector
    else:
        to_sector = [ring(me_s, d, sectors) for d in range(1, sectors)]
        from_sector = [ring(me_s, -d, sectors) for d in range(1, sectors)]
    sources = [me_s] + from_sector

    def slab(ag, s, t):
        return gath.at[ag, pl.ds(pl.multiple_of(s * width + t * rows, rows), rows)]

    def slab_copy(ag, s, t, to_s, to_t, k):
        here = slab(ag, s, t)
        return pltpu.make_async_remote_copy(
            src_ref=here, dst_ref=here,
            send_sem=ag_send.at[ag, k], recv_sem=ag_recv.at[ag, s * terms + t],
            device_id={"term": to_t, "sector": to_s}, device_id_type=MESH,
        )

    def arrive(ag, s, t):
        slab_copy(ag, s, t, ring(me_s, 1, sectors), me_t, 0).wait_recv()

    k_x = sectors - 1
    k_c = k_x + (chips - 1) * sectors
    n_send = k_c + chips * sectors

    def to_chips(ag, s, d):
        for e in range(1, chips):
            slab_copy(
                ag, s, me_t, me_s, term_at(ring(me_x, e, chips), me_c),
                k_x + (e - 1) * sectors + d,
            ).start()

    def to_core(ag, s, x, d, e):
        slab_copy(
            ag, s, term_at(x, me_c), me_s, term_at(me_x, other_c), k_c + e * sectors + d
        ).start()

    def gather_start(ag):
        for d in range(1, sectors):
            slab_copy(ag, me_s, me_t, to_sector[d - 1], me_t, d - 1).start()
        to_chips(ag, me_s, 0)
        to_core(ag, me_s, me_x, 0, 0)

    def gather_sector(ag):
        for d in range(1, sectors):
            s = sources[d]
            arrive(ag, s, me_t)
            to_chips(ag, s, d)
            to_core(ag, s, me_x, d, 0)

    def gather_chip(ag):
        for e in range(1, chips):
            x = ring(me_x, -e, chips)
            for d in range(sectors):
                s = sources[d]
                arrive(ag, s, term_at(x, me_c))
                to_core(ag, s, x, d, e)

    def gather_core(ag):
        for e in range(chips):
            x = ring(me_x, -e, chips)
            for d in range(sectors):
                arrive(ag, sources[d], term_at(x, other_c))

    def gather_rest(ag):
        gather_sector(ag)
        gather_chip(ag)
        gather_core(ag)

    def fold(value):
        return jnp.sum(value.reshape(CHUNK // 8, 8, width), axis=0)

    def chunk_of(i):
        return pl.ds(pl.multiple_of(i * CHUNK, CHUNK), CHUNK)

    def dots(pick, n):
        def body(i, sums):
            at = chunk_of(i)
            return tuple(a + fold(p) for a, p in zip(sums, pick(at)))

        zero = jnp.zeros((8, width), F32)
        sums = lax.fori_loop(0, steps, body, (zero,) * n, unroll=2)
        out = []
        for a in sums:
            a = jnp.sum(a, axis=0, keepdims=True)
            out.append(jnp.sum(a, axis=1, keepdims=True) / count)
        return out

    def put_x(i, value):
        high, low = split(value)
        block = i // per_block
        off = pl.multiple_of(lax.rem(i, per_block) * CHUNK, CHUNK)
        xcat[block, pl.ds(off, CHUNK), :] = high
        xcat[block, pl.ds(width + off, CHUNK), :] = low
        xcat[block, pl.ds(2 * width + off, CHUNK), :] = high

    def over_chunks(body):
        def step(i, carry):
            body(i, chunk_of(i))
            return carry

        lax.fori_loop(0, steps, step, 0, unroll=2)

    row_index = me_t * rows + lax.broadcasted_iota(jnp.int32, (rows, width), 0)
    col_index = lax.broadcasted_iota(jnp.int32, (rows, width), 1)
    live = (row_index < dims_ref[0]) & (col_index < dims_ref[1])
    mask = jnp.where(live, F32(1), F32(0))
    trial_load.wait()
    gath[first, own, :] = traw[...] * mask
    pl.semaphore_wait(barrier, len(others))
    gather_start(first)
    for load in loads:
        load.wait()
    xcat[sectors] = jnp.zeros((wide, width), BF16)

    def prepare(k, carry):
        high, low = split(lraw[k])
        lcat[k, :, 0:width] = high
        lcat[k, :, width : 2 * width] = high
        lcat[k, :, 2 * width :] = low
        high, low = split(rraw[k].T)
        base = pl.multiple_of(k * wide, wide)
        rcat[pl.ds(base, width), :] = high
        rcat[pl.ds(base + width, width), :] = low
        rcat[pl.ds(base + 2 * width, width), :] = high
        return carry

    gather_sector(first)
    lax.fori_loop(0, own_terms, prepare, 0)
    gather_chip(first)
    gather_core(first)
    pre_load.wait()
    gather_start(pre)

    (norm,) = dots(lambda at: (gath[first, at, :] * gath[first, at, :],), 1)
    scale = 1.0 / jnp.sqrt(norm + EPS)

    def begin(i, at):
        value = gath[first, at, :] * scale
        vec[at, :] = value
        put_x(i, value)

    over_chunks(begin)

    def rs_copy(it, d):
        to = ring(me_t, d, terms)
        return pltpu.make_async_remote_copy(
            src_ref=part.at[it, pl.ds(pl.multiple_of(to * rows, rows), rows)],
            dst_ref=rsbuf.at[it, d - 1],
            send_sem=rs_send.at[it, d - 1], recv_sem=rs_recv.at[it, d - 1],
            device_id={"term": to}, device_id_type=MESH,
        )

    def multiply(it):
        for k in range(own_terms):
            inner = jnp.dot(lcat[k], xcat[links_ref[k]], preferred_element_type=F32)
            high, low = split(inner)
            icat[:, k * wide : k * wide + width] = high
            icat[:, k * wide + width : k * wide + 2 * width] = high
            icat[:, k * wide + 2 * width : (k + 1) * wide] = low
        part[it] = jnp.dot(icat[...], rcat[...], preferred_element_type=F32)

    def rs_start(it):
        for d in range(1, terms):
            rs_copy(it, d).start()

    def collect(it):
        total = part[it, pl.ds(pl.multiple_of(me_t * rows, rows), rows), :]
        for d in range(1, terms):
            rs_copy(it, d).wait_recv()
            total = total + rsbuf[it, d - 1]
        gath[it, own, :] = total * mask
        gather_start(it)

    multiply(0)
    rs_start(0)
    gather_sector(pre)
    collect(0)
    gather_chip(pre)
    gather_core(pre)

    def invert(i, at):
        pinv[at, :] = 1.0 / gath[pre, at, :]

    over_chunks(invert)
    gather_rest(0)
    (theta,) = dots(lambda at: (vec[at, :] * gath[0, at, :],), 1)

    def begin_residual(i, at):
        w = gath[0, at, :]
        img[at, :] = w
        r = (w - theta * vec[at, :]) * pinv[at, :]
        res[at, :] = r
        put_x(i, r)

    over_chunks(begin_residual)

    def early(at):
        v, w, r = vec[at, :], img[at, :], res[at, :]
        return v * v, v * w, v * r, r * r, r * w

    def rotate(theta, vv, vw, along, rr, rw, vh, rh):
        proj = rr - 2.0 * along * along + along * along * vv
        g = 1.0 / jnp.sqrt(proj + EPS)
        cross = 0.5 * g * ((vh - along * vw) + (rw - along * vw))
        diag_c = g * g * (rh - along * (rw + vh) + along * along * vw)
        half = 0.5 * (theta - diag_c)
        spread = jnp.sqrt(half * half + cross * cross)
        lowest = 0.5 * (theta + diag_c) - spread
        coef_x = spread - half
        coef_y = -cross
        length = jnp.sqrt(coef_x * coef_x + coef_y * coef_y)
        c_new = coef_y * g / length
        c_old = (coef_x - coef_y * g * along) / length
        return lowest, c_old, c_new

    def iterate(it, theta):
        multiply(it)
        rs_start(it)
        known = dots(early, 5)
        collect(it)
        gather_rest(it)

        def late(at):
            h = gath[it, at, :]
            return vec[at, :] * h, res[at, :] * h

        vh, rh = dots(late, 2)
        lowest, c_old, c_new = rotate(theta, *known, vh, rh)

        def update(i, at):
            v = c_old * vec[at, :] + c_new * res[at, :]
            w = c_old * img[at, :] + c_new * gath[it, at, :]
            vec[at, :] = v
            img[at, :] = w
            r = (w - lowest * v) * pinv[at, :]
            res[at, :] = r
            put_x(i, r)

        over_chunks(update)
        return lowest

    theta = lax.fori_loop(1, ITERS, iterate, theta)

    multiply(ITERS)
    me = me_s * terms + me_t

    def sc_copy(k):
        a, b = others[k]
        return pltpu.make_async_remote_copy(
            src_ref=scal.at[me], dst_ref=scal.at[me],
            send_sem=sc_send.at[k], recv_sem=sc_recv.at[me],
            device_id={"term": ring(me_t, b, terms), "sector": ring(me_s, a, sectors)},
            device_id_type=MESH,
        )

    vh, rh = jnp.zeros((8, width), F32), jnp.zeros((8, width), F32)
    for i in range(per_block):
        at = pl.ds(pl.multiple_of(me_s * width + i * CHUNK, CHUNK), CHUNK)
        h = part[ITERS, i * CHUNK : (i + 1) * CHUNK, :]
        vh = vh + fold(vec[at, :] * h)
        rh = rh + fold(res[at, :] * h)
    scal[me, 0:8, :] = vh
    scal[me, 8:16, :] = rh
    for k in range(len(others)):
        sc_copy(k).start()
    known = dots(early, 5)
    for a, b in others:
        source = ring(me_s, a, sectors) * terms + ring(me_t, b, terms)
        pltpu.make_async_remote_copy(
            src_ref=scal.at[source], dst_ref=scal.at[source],
            send_sem=sc_send.at[0], recv_sem=sc_recv.at[source],
            device_id={"sector": ring(me_s, 1, sectors)}, device_id_type=MESH,
        ).wait_recv()
    sums = jnp.sum(scal[...], axis=0)

    def whole_sum(value):
        value = jnp.sum(value, axis=0, keepdims=True)
        return jnp.sum(value, axis=1, keepdims=True) / count

    theta, c_old, c_new = rotate(theta, *known, whole_sum(sums[0:8]), whole_sum(sums[8:16]))
    ground_ref[...] = c_old * vec[own, :] + c_new * res[own, :]
    energy_ref[...] = jnp.broadcast_to(theta, energy_ref.shape)

    def finish(ag, carry):
        for k in range(n_send):
            slab_copy(ag, me_s, me_t, ring(me_s, 1, sectors), me_t, k).wait_send()
        return carry

    lax.fori_loop(0, ITERS + 2, finish, 0)

    def finish_rs(it, carry):
        for d in range(1, terms):
            rs_copy(it, d).wait_send()
        return carry

    lax.fori_loop(0, ITERS, finish_rs, 0)
    for k in range(len(others)):
        sc_copy(k).wait_send()


def on_device(trial, precond, left_ops, right_ops, links, block_dims):
    sectors = lax.axis_size("sector")
    terms = lax.axis_size("term")
    _, rows, width = trial.shape
    own_terms = left_ops.shape[0]
    count = float(sectors * width * width)
    applies = ITERS + 1
    gathers = ITERS + 2
    whole = (sectors * width, width)
    vmem = pl.BlockSpec(memory_space=pltpu.VMEM)
    smem = pl.BlockSpec(memory_space=pltpu.SMEM)
    hbm = pl.BlockSpec(memory_space=pltpu.HBM)
    ground, energy = pl.pallas_call(
        functools.partial(kernel, sectors, terms, count),
        out_shape=(
            jax.ShapeDtypeStruct((rows, width), F32),
            jax.ShapeDtypeStruct((1, 128), F32),
        ),
        in_specs=[smem, smem, hbm, hbm, hbm, hbm],
        out_specs=(vmem, vmem),
        scratch_shapes=[
            pltpu.VMEM((gathers,) + whole, F32),
            pltpu.VMEM((applies, width, width), F32),
            pltpu.VMEM((ITERS, terms - 1, rows, width), F32),
            pltpu.VMEM(whole, F32),
            pltpu.VMEM(whole, F32),
            pltpu.VMEM(whole, F32),
            pltpu.VMEM(whole, F32),
            pltpu.VMEM((sectors + 1, 3 * width, width), BF16),
            pltpu.VMEM((own_terms, width, 3 * width), BF16),
            pltpu.VMEM((own_terms * 3 * width, width), BF16),
            pltpu.VMEM((width, own_terms * 3 * width), BF16),
            pltpu.VMEM((own_terms, width, width), F32),
            pltpu.VMEM((own_terms, width, width), F32),
            pltpu.VMEM((rows, width), F32),
            pltpu.VMEM((sectors * terms, 16, width), F32),
            pltpu.SemaphoreType.DMA((gathers, sectors * terms)),
            pltpu.SemaphoreType.DMA((gathers, sectors * terms)),
            pltpu.SemaphoreType.DMA((ITERS, terms - 1)),
            pltpu.SemaphoreType.DMA((ITERS, terms - 1)),
            pltpu.SemaphoreType.DMA((sectors * terms,)),
            pltpu.SemaphoreType.DMA((sectors * terms,)),
            pltpu.SemaphoreType.DMA((4,)),
        ],
        compiler_params=pltpu.CompilerParams(
            collective_id=0, has_side_effects=True, vmem_limit_bytes=52 * 2**20
        ),
    )(
        links.reshape(own_terms),
        block_dims.reshape(2),
        trial.reshape(rows, width),
        precond.reshape(rows, width),
        left_ops.reshape(own_terms, width, width),
        right_ops.reshape(own_terms, width, width),
    )
    return ground.reshape(1, rows, width), energy[0, :1]


def solution(mesh):
    in_specs = (
        P(("group", "sector"), "term", None),
        P(("group", "sector"), "term", None),
        P(("group", "term"), "sector", None, None),
        P(("group", "term"), "sector", None, None),
        P(("group", "term"), "sector"),
        P(("group", "sector"), None),
    )
    out_specs = (P(("group", "sector"), "term", None), P("group"))
    return jax.shard_map(
        on_device, mesh=mesh, in_specs=in_specs, out_specs=out_specs, check_vma=False
    )
```

```python
import functools

import jax
import jax.numpy as jnp
from jax import lax
from jax.experimental import pallas as pl
from jax.experimental.pallas import tpu as pltpu
from jax.sharding import PartitionSpec as P

ITERS = 3
EPS = 1e-06
CORES = 2
CHUNK = 64
PARTS = 1
MESH = pl.DeviceIdType.MESH
F32 = jnp.float32
BF16 = jnp.bfloat16


def split(value):
    high = value.astype(BF16)
    low = (value - high.astype(F32)).astype(BF16)
    return high, low


def kernel(
    sectors, terms, count,
    links_hbm, dims_hbm, trial_ref, pre_ref, left_ref, right_ref,
    ground_ref, energy_ref,
    gath, part, rsbuf, vec, img, res, pinv, xcat, lcat, rcat, icat, lraw, rraw, traw, scal, links_ref, dims_ref,
    ag_send, ag_recv, rs_send, rs_recv, sc_send, sc_recv, load_sem,
):
    rows, width = traw.shape
    own_terms = lraw.shape[0]
    chips = terms // CORES
    me_t = lax.axis_index("term")
    me_s = lax.axis_index("sector")
    me_x = me_t // CORES
    me_c = lax.rem(me_t, CORES)
    other_c = (CORES - 1) - me_c
    wide = 3 * width
    quad = sectors == 4 and terms == 2 * CORES
    parts = PARTS if quad else 1
    piece = rows // parts
    total_rows = sectors * width
    steps = total_rows // CHUNK
    per_block = width // CHUNK

    def term_at(x, c):
        return x * CORES + c

    def ring(i, d, n):
        return lax.rem(i + d + n, n)

    others = [(a, b) for a in range(sectors) for b in range(terms) if a or b]
    barrier = pltpu.get_barrier_semaphore()
    for a, b in others:
        pl.semaphore_signal(
            barrier, inc=1,
            device_id={"term": ring(me_t, b, terms), "sector": ring(me_s, a, sectors)},
            device_id_type=MESH,
        )
    first, pre = ITERS, ITERS + 1
    own = pl.ds(pl.multiple_of(me_s * width + me_t * rows, rows), rows)
    trial_load = pltpu.make_async_copy(trial_ref, traw, load_sem.at[2])
    pre_load = pltpu.make_async_copy(pre_ref, gath.at[pre, own], load_sem.at[3])
    loads = [
        pltpu.make_async_copy(left_ref, lraw, load_sem.at[0]),
        pltpu.make_async_copy(right_ref, rraw, load_sem.at[1]),
    ]
    small = [
        pltpu.make_async_copy(dims_hbm, dims_ref, load_sem.at[4]),
        pltpu.make_async_copy(links_hbm, links_ref, load_sem.at[5]),
    ]
    trial_load.start()
    for load in small:
        load.start()
    for load in loads:
        load.start()
    pre_load.start()

    def slab(ag, s, t, p):
        at = s * width + t * rows + p * piece
        return gath.at[ag, pl.ds(pl.multiple_of(at, piece), piece)]

    def slab_copy(ag, s, t, p, to_s, to_t, k):
        here = slab(ag, s, t, p)
        return pltpu.make_async_remote_copy(
            src_ref=here, dst_ref=here,
            send_sem=ag_send.at[ag, k], recv_sem=ag_recv.at[ag, (s * terms + t) * parts + p],
            device_id={"term": to_t, "sector": to_s}, device_id_type=MESH,
        )

    def arrive(ag, s, t, p):
        slab_copy(ag, s, t, p, ring(me_s, 1, sectors), me_t, 0).wait_recv()

    n_send = (sectors * terms - 1) * parts

    if quad:
        near_s = [me_s, me_s + 1 - 2 * lax.rem(me_s, 2), lax.rem(me_s + 2, 4), 3 - me_s]
        near_x = [me_x, 1 - me_x]
        near_c = [me_c, other_c]

        def place(rel):
            return near_s[rel[0]], term_at(near_x[rel[1]], near_c[rel[2]])

        here, core, chip, near, diag = (0, 0, 0), (0, 0, 1), (0, 1, 0), (1, 0, 0), (1, 1, 0)
        across, far = (2, 0, 0), (3, 1, 0)
        after = [chip, near, diag, (2, 1, 0), (3, 0, 0), far]
        begin_plan = [(here, to) for to in (across, chip, near, diag, far)] + [(here, core)]
        relay_plan = [(across, to) for to in (chip, near)] + [(across, core)]
        sends = [(a, to, p) for a, to in begin_plan + relay_plan for p in range(parts)]
        sends += [(a, core, p) for a in after for p in range(parts)]
        index = {send: k for k, send in enumerate(sends)}

        def push(ag, a, to, p):
            slab_copy(ag, *place(a), p, *place(to), index[a, to, p]).start()

        def gather_start(ag):
            for a, to in begin_plan:
                for p in range(parts):
                    push(ag, a, to, p)

        def gather_relay(ag):
            for p in range(parts):
                arrive(ag, *place(across), p)
                for a, to in relay_plan:
                    push(ag, a, to, p)

        def gather_finish(ag):
            for a in after:
                for p in range(parts):
                    arrive(ag, *place(a), p)
                    push(ag, a, core, p)
            for a in [here, across] + after:
                for p in range(parts):
                    arrive(ag, *place((a[0], a[1], 1)), p)
    else:
        k_x = sectors - 1
        k_c = k_x + (chips - 1) * sectors

        def to_chips(ag, s, d):
            for e in range(1, chips):
                slab_copy(
                    ag, s, me_t, 0, me_s, term_at(ring(me_x, e, chips), me_c),
                    k_x + (e - 1) * sectors + d,
                ).start()

        def to_core(ag, s, x, d, e):
            slab_copy(
                ag, s, term_at(x, me_c), 0, me_s, term_at(me_x, other_c),
                k_c + e * sectors + d,
            ).start()

        def gather_start(ag):
            for d in range(1, sectors):
                slab_copy(ag, me_s, me_t, 0, ring(me_s, d, sectors), me_t, d - 1).start()
            to_chips(ag, me_s, 0)
            to_core(ag, me_s, me_x, 0, 0)

        def gather_relay(ag):
            for d in range(1, sectors):
                s = ring(me_s, -d, sectors)
                arrive(ag, s, me_t, 0)
                to_chips(ag, s, d)
                to_core(ag, s, me_x, d, 0)

        def gather_finish(ag):
            for e in range(1, chips):
                x = ring(me_x, -e, chips)
                for d in range(sectors):
                    s = ring(me_s, -d, sectors)
                    arrive(ag, s, term_at(x, me_c), 0)
                    to_core(ag, s, x, d, e)
            for e in range(chips):
                x = ring(me_x, -e, chips)
                for d in range(sectors):
                    arrive(ag, ring(me_s, -d, sectors), term_at(x, other_c), 0)

    def fold(value):
        return jnp.sum(value.reshape(CHUNK // 8, 8, width), axis=0)

    def chunk_of(i):
        return pl.ds(pl.multiple_of(i * CHUNK, CHUNK), CHUNK)

    def dots(pick, n):
        def body(i, sums):
            at = chunk_of(i)
            return tuple(a + fold(p) for a, p in zip(sums, pick(at)))

        zero = jnp.zeros((8, width), F32)
        sums = lax.fori_loop(0, steps, body, (zero,) * n, unroll=2)
        out = []
        for a in sums:
            a = jnp.sum(a, axis=0, keepdims=True)
            out.append(jnp.sum(a, axis=1, keepdims=True) / count)
        return out

    def put_x(i, value):
        high, low = split(value)
        block = i // per_block
        off = pl.multiple_of(lax.rem(i, per_block) * CHUNK, CHUNK)
        xcat[block, pl.ds(off, CHUNK), :] = high
        xcat[block, pl.ds(width + off, CHUNK), :] = low
        xcat[block, pl.ds(2 * width + off, CHUNK), :] = high

    def over_chunks(body):
        def step(i, carry):
            body(i, chunk_of(i))
            return carry

        lax.fori_loop(0, steps, step, 0, unroll=2)

    for load in small:
        load.wait()
    row_index = me_t * rows + lax.broadcasted_iota(jnp.int32, (rows, width), 0)
    col_index = lax.broadcasted_iota(jnp.int32, (rows, width), 1)
    live = (row_index < dims_ref[0]) & (col_index < dims_ref[1])
    mask = jnp.where(live, F32(1), F32(0))
    trial_load.wait()
    gath[first, own, :] = traw[...] * mask
    pl.semaphore_wait(barrier, len(others))
    gather_start(first)
    for load in loads:
        load.wait()
    xcat[sectors] = jnp.zeros((wide, width), BF16)

    def prepare(k, carry):
        high, low = split(lraw[k])
        lcat[k, :, 0:width] = high
        lcat[k, :, width : 2 * width] = high
        lcat[k, :, 2 * width :] = low
        high, low = split(rraw[k].T)
        base = pl.multiple_of(k * wide, wide)
        rcat[pl.ds(base, width), :] = high
        rcat[pl.ds(base + width, width), :] = low
        rcat[pl.ds(base + 2 * width, width), :] = high
        return carry

    gather_relay(first)
    lax.fori_loop(0, own_terms, prepare, 0)
    gather_finish(first)
    pre_load.wait()
    gather_start(pre)

    (norm,) = dots(lambda at: (gath[first, at, :] * gath[first, at, :],), 1)
    scale = 1.0 / jnp.sqrt(norm + EPS)

    def begin(i, at):
        value = gath[first, at, :] * scale
        vec[at, :] = value
        put_x(i, value)

    over_chunks(begin)

    def rs_copy(it, d):
        to = ring(me_t, d, terms)
        return pltpu.make_async_remote_copy(
            src_ref=part.at[it, pl.ds(pl.multiple_of(to * rows, rows), rows)],
            dst_ref=rsbuf.at[it, d - 1],
            send_sem=rs_send.at[it, d - 1], recv_sem=rs_recv.at[it, d - 1],
            device_id={"term": to}, device_id_type=MESH,
        )

    def multiply(it):
        for k in range(own_terms):
            inner = jnp.dot(lcat[k], xcat[links_ref[k]], preferred_element_type=F32)
            high, low = split(inner)
            icat[:, k * wide : k * wide + width] = high
            icat[:, k * wide + width : k * wide + 2 * width] = high
            icat[:, k * wide + 2 * width : (k + 1) * wide] = low
        part[it] = jnp.dot(icat[...], rcat[...], preferred_element_type=F32)

    def rs_start(it):
        for d in range(1, terms):
            rs_copy(it, d).start()

    def collect(it):
        total = part[it, pl.ds(pl.multiple_of(me_t * rows, rows), rows), :]
        for d in range(1, terms):
            rs_copy(it, d).wait_recv()
            total = total + rsbuf[it, d - 1]
        gath[it, own, :] = total * mask
        gather_start(it)

    multiply(0)
    rs_start(0)
    gather_relay(pre)
    collect(0)
    gather_finish(pre)

    def invert(i, at):
        pinv[at, :] = 1.0 / gath[pre, at, :]

    over_chunks(invert)
    gather_relay(0)
    gather_finish(0)
    (theta,) = dots(lambda at: (vec[at, :] * gath[0, at, :],), 1)

    def begin_residual(i, at):
        w = gath[0, at, :]
        img[at, :] = w
        r = (w - theta * vec[at, :]) * pinv[at, :]
        res[at, :] = r
        put_x(i, r)

    over_chunks(begin_residual)

    def early(at):
        v, w, r = vec[at, :], img[at, :], res[at, :]
        return v * v, v * w, v * r, r * r, r * w

    def rotate(theta, vv, vw, along, rr, rw, vh, rh):
        proj = rr - 2.0 * along * along + along * along * vv
        g = 1.0 / jnp.sqrt(proj + EPS)
        cross = 0.5 * g * ((vh - along * vw) + (rw - along * vw))
        diag_c = g * g * (rh - along * (rw + vh) + along * along * vw)
        half = 0.5 * (theta - diag_c)
        spread = jnp.sqrt(half * half + cross * cross)
        lowest = 0.5 * (theta + diag_c) - spread
        coef_x = spread - half
        coef_y = -cross
        length = jnp.sqrt(coef_x * coef_x + coef_y * coef_y)
        c_new = coef_y * g / length
        c_old = (coef_x - coef_y * g * along) / length
        return lowest, c_old, c_new

    def iterate(it, theta):
        multiply(it)
        rs_start(it)
        known = dots(early, 5)
        collect(it)
        gather_relay(it)
        gather_finish(it)

        def late(at):
            h = gath[it, at, :]
            return vec[at, :] * h, res[at, :] * h

        vh, rh = dots(late, 2)
        lowest, c_old, c_new = rotate(theta, *known, vh, rh)

        def update(i, at):
            v = c_old * vec[at, :] + c_new * res[at, :]
            w = c_old * img[at, :] + c_new * gath[it, at, :]
            vec[at, :] = v
            img[at, :] = w
            r = (w - lowest * v) * pinv[at, :]
            res[at, :] = r
            put_x(i, r)

        over_chunks(update)
        return lowest

    theta = lax.fori_loop(1, ITERS, iterate, theta)

    multiply(ITERS)
    me = me_s * terms + me_t

    def sc_copy(k):
        a, b = others[k]
        return pltpu.make_async_remote_copy(
            src_ref=scal.at[me], dst_ref=scal.at[me],
            send_sem=sc_send.at[k], recv_sem=sc_recv.at[me],
            device_id={"term": ring(me_t, b, terms), "sector": ring(me_s, a, sectors)},
            device_id_type=MESH,
        )

    vh, rh = jnp.zeros((8, width), F32), jnp.zeros((8, width), F32)
    for i in range(per_block):
        at = pl.ds(pl.multiple_of(me_s * width + i * CHUNK, CHUNK), CHUNK)
        h = part[ITERS, i * CHUNK : (i + 1) * CHUNK, :]
        vh = vh + fold(vec[at, :] * h)
        rh = rh + fold(res[at, :] * h)
    scal[me, 0:8, :] = vh
    scal[me, 8:16, :] = rh
    for k in range(len(others)):
        sc_copy(k).start()
    known = dots(early, 5)
    for a, b in others:
        source = ring(me_s, a, sectors) * terms + ring(me_t, b, terms)
        pltpu.make_async_remote_copy(
            src_ref=scal.at[source], dst_ref=scal.at[source],
            send_sem=sc_send.at[0], recv_sem=sc_recv.at[source],
            device_id={"sector": ring(me_s, 1, sectors)}, device_id_type=MESH,
        ).wait_recv()
    sums = jnp.sum(scal[...], axis=0)

    def whole_sum(value):
        value = jnp.sum(value, axis=0, keepdims=True)
        return jnp.sum(value, axis=1, keepdims=True) / count

    theta, c_old, c_new = rotate(theta, *known, whole_sum(sums[0:8]), whole_sum(sums[8:16]))
    ground_ref[...] = c_old * vec[own, :] + c_new * res[own, :]
    energy_ref[...] = jnp.broadcast_to(theta, energy_ref.shape)

    def finish(ag, carry):
        for k in range(n_send):
            slab_copy(ag, me_s, me_t, 0, ring(me_s, 1, sectors), me_t, k).wait_send()
        return carry

    lax.fori_loop(0, ITERS + 2, finish, 0)

    def finish_rs(it, carry):
        for d in range(1, terms):
            rs_copy(it, d).wait_send()
        return carry

    lax.fori_loop(0, ITERS, finish_rs, 0)
    for k in range(len(others)):
        sc_copy(k).wait_send()


def on_device(trial, precond, left_ops, right_ops, links, block_dims):
    sectors = lax.axis_size("sector")
    terms = lax.axis_size("term")
    _, rows, width = trial.shape
    own_terms = left_ops.shape[0]
    count = float(sectors * width * width)
    applies = ITERS + 1
    gathers = ITERS + 2
    whole = (sectors * width, width)
    vmem = pl.BlockSpec(memory_space=pltpu.VMEM)
    hbm = pl.BlockSpec(memory_space=pltpu.HBM)
    ground, energy = pl.pallas_call(
        functools.partial(kernel, sectors, terms, count),
        out_shape=(
            jax.ShapeDtypeStruct((rows, width), F32),
            jax.ShapeDtypeStruct((1, 128), F32),
        ),
        in_specs=[hbm] * 6,
        out_specs=(vmem, vmem),
        scratch_shapes=[
            pltpu.VMEM((gathers,) + whole, F32),
            pltpu.VMEM((applies, width, width), F32),
            pltpu.VMEM((ITERS, terms - 1, rows, width), F32),
            pltpu.VMEM(whole, F32),
            pltpu.VMEM(whole, F32),
            pltpu.VMEM(whole, F32),
            pltpu.VMEM(whole, F32),
            pltpu.VMEM((sectors + 1, 3 * width, width), BF16),
            pltpu.VMEM((own_terms, width, 3 * width), BF16),
            pltpu.VMEM((own_terms * 3 * width, width), BF16),
            pltpu.VMEM((width, own_terms * 3 * width), BF16),
            pltpu.VMEM((own_terms, width, width), F32),
            pltpu.VMEM((own_terms, width, width), F32),
            pltpu.VMEM((rows, width), F32),
            pltpu.VMEM((sectors * terms, 16, width), F32),
            pltpu.SMEM((own_terms,), jnp.int32),
            pltpu.SMEM((2,), jnp.int32),
            pltpu.SemaphoreType.DMA((gathers, sectors * terms * PARTS)),
            pltpu.SemaphoreType.DMA((gathers, sectors * terms * PARTS)),
            pltpu.SemaphoreType.DMA((ITERS, terms - 1)),
            pltpu.SemaphoreType.DMA((ITERS, terms - 1)),
            pltpu.SemaphoreType.DMA((sectors * terms,)),
            pltpu.SemaphoreType.DMA((sectors * terms,)),
            pltpu.SemaphoreType.DMA((6,)),
        ],
        compiler_params=pltpu.CompilerParams(
            collective_id=0, has_side_effects=True, vmem_limit_bytes=60 * 2**20
        ),
    )(
        links.reshape(own_terms),
        block_dims.reshape(2),
        trial.reshape(rows, width),
        precond.reshape(rows, width),
        left_ops.reshape(own_terms, width, width),
        right_ops.reshape(own_terms, width, width),
    )
    return ground.reshape(1, rows, width), energy[0, :1]


def solution(mesh):
    in_specs = (
        P(("group", "sector"), "term", None),
        P(("group", "sector"), "term", None),
        P(("group", "term"), "sector", None, None),
        P(("group", "term"), "sector", None, None),
        P(("group", "term"), "sector"),
        P(("group", "sector"), None),
    )
    out_specs = (P(("group", "sector"), "term", None), P("group"))
    return jax.shard_map(
        on_device, mesh=mesh, in_specs=in_specs, out_specs=out_specs, check_vma=False
    )
```

```python
import functools

import jax
import jax.numpy as jnp
from jax import lax
from jax.experimental import pallas as pl
from jax.experimental.pallas import tpu as pltpu
from jax.sharding import PartitionSpec as P

ITERS = 3
EPS = 1e-06
CORES = 2
CHUNK = 64
PARTS = 1
MESH = pl.DeviceIdType.MESH
F32 = jnp.float32
BF16 = jnp.bfloat16


def split(value):
    high = value.astype(BF16)
    low = (value - high.astype(F32)).astype(BF16)
    return high, low


def kernel(
    sectors, terms, count,
    links_hbm, dims_hbm, trial_ref, pre_ref, left_ref, right_ref,
    ground_ref, energy_ref,
    gath, part, rsbuf, vec, img, res, pinv, xcat, lcat, rcat, icat, lraw, rraw, traw, scal, links_ref, dims_ref,
    ag_send, ag_recv, rs_send, rs_recv, sc_send, sc_recv, load_sem,
):
    rows, width = traw.shape
    own_terms = lraw.shape[0]
    chips = terms // CORES
    me_t = lax.axis_index("term")
    me_s = lax.axis_index("sector")
    me_x = me_t // CORES
    me_c = lax.rem(me_t, CORES)
    other_c = (CORES - 1) - me_c
    wide = 3 * width
    quad = sectors == 4 and terms == 2 * CORES
    parts = PARTS if quad else 1
    piece = rows // parts
    total_rows = sectors * width
    steps = total_rows // CHUNK
    per_block = width // CHUNK

    def term_at(x, c):
        return x * CORES + c

    def ring(i, d, n):
        return lax.rem(i + d + n, n)

    others = [(a, b) for a in range(sectors) for b in range(terms) if a or b]
    barrier = pltpu.get_barrier_semaphore()
    for a, b in others:
        pl.semaphore_signal(
            barrier, inc=1,
            device_id={"term": ring(me_t, b, terms), "sector": ring(me_s, a, sectors)},
            device_id_type=MESH,
        )
    first, pre = ITERS, ITERS + 1
    own = pl.ds(pl.multiple_of(me_s * width + me_t * rows, rows), rows)
    trial_load = pltpu.make_async_copy(trial_ref, traw, load_sem.at[2])
    pre_load = pltpu.make_async_copy(pre_ref, gath.at[pre, own], load_sem.at[3])
    loads = [
        pltpu.make_async_copy(left_ref, lraw, load_sem.at[0]),
        pltpu.make_async_copy(right_ref, rraw, load_sem.at[1]),
    ]
    small = [
        pltpu.make_async_copy(dims_hbm, dims_ref, load_sem.at[4]),
        pltpu.make_async_copy(links_hbm, links_ref, load_sem.at[5]),
    ]
    trial_load.start()
    for load in small:
        load.start()
    for load in loads:
        load.start()
    pre_load.start()

    def slab(ag, s, t, p):
        at = s * width + t * rows + p * piece
        return gath.at[ag, pl.ds(pl.multiple_of(at, piece), piece)]

    def slab_copy(ag, s, t, p, to_s, to_t):
        here = slab(ag, s, t, p)
        return pltpu.make_async_remote_copy(
            src_ref=here, dst_ref=here,
            send_sem=ag_send.at[ag], recv_sem=ag_recv.at[ag, (s * terms + t) * parts + p],
            device_id={"term": to_t, "sector": to_s}, device_id_type=MESH,
        )

    def arrive(ag, s, t, p):
        slab_copy(ag, s, t, p, ring(me_s, 1, sectors), me_t).wait_recv()

    def sent(ref, sem):
        pltpu.make_async_remote_copy(
            src_ref=ref, dst_ref=ref, send_sem=sem, recv_sem=ag_recv.at[0, 0],
            device_id={"sector": ring(me_s, 1, sectors)}, device_id_type=MESH,
        ).wait_send()

    def gather_sent(ag):
        sent(gath.at[ag, pl.ds(0, (sectors * terms - 1) * rows)], ag_send.at[ag])


    if quad:
        near_s = [me_s, me_s + 1 - 2 * lax.rem(me_s, 2), lax.rem(me_s + 2, 4), 3 - me_s]
        near_x = [me_x, 1 - me_x]
        near_c = [me_c, other_c]

        def place(rel):
            return near_s[rel[0]], term_at(near_x[rel[1]], near_c[rel[2]])

        here, core, chip, near, diag = (0, 0, 0), (0, 0, 1), (0, 1, 0), (1, 0, 0), (1, 1, 0)
        across, far = (2, 0, 0), (3, 1, 0)
        after = [chip, near, diag, (2, 1, 0), (3, 0, 0), far]
        begin_plan = [(here, to) for to in (across, chip, near, diag, far)] + [(here, core)]
        relay_plan = [(across, to) for to in (chip, near)] + [(across, core)]

        def push(ag, a, to, p):
            slab_copy(ag, *place(a), p, *place(to)).start()

        def gather_start(ag):
            for a, to in begin_plan:
                for p in range(parts):
                    push(ag, a, to, p)

        def gather_relay(ag):
            for p in range(parts):
                arrive(ag, *place(across), p)
                for a, to in relay_plan:
                    push(ag, a, to, p)

        def gather_finish(ag):
            for a in after:
                for p in range(parts):
                    arrive(ag, *place(a), p)
                    push(ag, a, core, p)
            for a in [here, across] + after:
                for p in range(parts):
                    arrive(ag, *place((a[0], a[1], 1)), p)
    else:
        def to_chips(ag, s):
            for e in range(1, chips):
                slab_copy(
                    ag, s, me_t, 0, me_s, term_at(ring(me_x, e, chips), me_c)
                ).start()

        def to_core(ag, s, x):
            slab_copy(
                ag, s, term_at(x, me_c), 0, me_s, term_at(me_x, other_c)
            ).start()

        def gather_start(ag):
            for d in range(1, sectors):
                slab_copy(ag, me_s, me_t, 0, ring(me_s, d, sectors), me_t).start()
            to_chips(ag, me_s)
            to_core(ag, me_s, me_x)

        def gather_relay(ag):
            for d in range(1, sectors):
                s = ring(me_s, -d, sectors)
                arrive(ag, s, me_t, 0)
                to_chips(ag, s)
                to_core(ag, s, me_x)

        def gather_finish(ag):
            for e in range(1, chips):
                x = ring(me_x, -e, chips)
                for d in range(sectors):
                    s = ring(me_s, -d, sectors)
                    arrive(ag, s, term_at(x, me_c), 0)
                    to_core(ag, s, x)
            for e in range(chips):
                x = ring(me_x, -e, chips)
                for d in range(sectors):
                    arrive(ag, ring(me_s, -d, sectors), term_at(x, other_c), 0)

    def fold(value):
        return jnp.sum(value.reshape(CHUNK // 8, 8, width), axis=0)

    def chunk_of(i):
        return pl.ds(pl.multiple_of(i * CHUNK, CHUNK), CHUNK)

    def dots(pick, n):
        def body(i, sums):
            at = chunk_of(i)
            return tuple(a + fold(p) for a, p in zip(sums, pick(at)))

        zero = jnp.zeros((8, width), F32)
        sums = lax.fori_loop(0, steps, body, (zero,) * n, unroll=2)
        out = []
        for a in sums:
            a = jnp.sum(a, axis=0, keepdims=True)
            out.append(jnp.sum(a, axis=1, keepdims=True) / count)
        return out

    def put_x(i, value):
        high, low = split(value)
        block = i // per_block
        off = pl.multiple_of(lax.rem(i, per_block) * CHUNK, CHUNK)
        xcat[block, pl.ds(off, CHUNK), :] = high
        xcat[block, pl.ds(width + off, CHUNK), :] = low
        xcat[block, pl.ds(2 * width + off, CHUNK), :] = high

    def over_chunks(body):
        def step(i, carry):
            body(i, chunk_of(i))
            return carry

        lax.fori_loop(0, steps, step, 0, unroll=2)

    for load in small:
        load.wait()
    row_index = me_t * rows + lax.broadcasted_iota(jnp.int32, (rows, width), 0)
    col_index = lax.broadcasted_iota(jnp.int32, (rows, width), 1)
    live = (row_index < dims_ref[0]) & (col_index < dims_ref[1])
    mask = jnp.where(live, F32(1), F32(0))
    trial_load.wait()
    gath[first, own, :] = traw[...] * mask
    pl.semaphore_wait(barrier, len(others))
    gather_start(first)
    for load in loads:
        load.wait()
    xcat[sectors] = jnp.zeros((wide, width), BF16)

    def prepare(k, carry):
        high, low = split(lraw[k])
        lcat[k, :, 0:width] = high
        lcat[k, :, width : 2 * width] = high
        lcat[k, :, 2 * width :] = low
        high, low = split(rraw[k].T)
        base = pl.multiple_of(k * wide, wide)
        rcat[pl.ds(base, width), :] = high
        rcat[pl.ds(base + width, width), :] = low
        rcat[pl.ds(base + 2 * width, width), :] = high
        return carry

    gather_relay(first)
    lax.fori_loop(0, own_terms, prepare, 0)
    gather_finish(first)
    pre_load.wait()
    gather_start(pre)
    gather_sent(first)

    (norm,) = dots(lambda at: (gath[first, at, :] * gath[first, at, :],), 1)
    scale = 1.0 / jnp.sqrt(norm + EPS)

    def begin(i, at):
        value = gath[first, at, :] * scale
        vec[at, :] = value
        put_x(i, value)

    over_chunks(begin)

    if quad:
        rows_to = [term_at(1 - me_x, me_c), term_at(1 - me_x, other_c), term_at(me_x, other_c)]
    else:
        rows_to = [ring(me_t, d, terms) for d in range(1, terms)]

    def rs_copy(it, d):
        to = rows_to[d - 1]
        return pltpu.make_async_remote_copy(
            src_ref=part.at[it, pl.ds(pl.multiple_of(to * rows, rows), rows)],
            dst_ref=rsbuf.at[it, d - 1],
            send_sem=rs_send.at[it, d - 1], recv_sem=rs_recv.at[it, d - 1],
            device_id={"term": to}, device_id_type=MESH,
        )

    def multiply(it, last=False):
        for k in range(own_terms):
            inner = jnp.dot(lcat[k], xcat[links_ref[k]], preferred_element_type=F32)
            high, low = split(inner)
            icat[:, k * wide : k * wide + width] = high
            icat[:, k * wide + width : k * wide + 2 * width] = high
            icat[:, k * wide + 2 * width : (k + 1) * wide] = low
        if quad and not last:
            for x, sends in ((1 - me_x, (1, 2)), (me_x, (3,))):
                at = pl.ds(pl.multiple_of(x * (width // 2), width // 2), width // 2)
                part[it, at, :] = jnp.dot(icat[at, :], rcat[...], preferred_element_type=F32)
                for d in sends:
                    rs_copy(it, d).start()
            return
        part[it] = jnp.dot(icat[...], rcat[...], preferred_element_type=F32)
        if not last:
            for d in range(1, terms):
                rs_copy(it, d).start()

    def collect(it):
        total = part[it, pl.ds(pl.multiple_of(me_t * rows, rows), rows), :]
        for d in range(1, terms):
            rs_copy(it, d).wait_recv()
            total = total + rsbuf[it, d - 1]
        gath[it, own, :] = total * mask
        gather_start(it)

    multiply(0)
    gather_relay(pre)
    collect(0)
    gather_finish(pre)

    def invert(i, at):
        pinv[at, :] = 1.0 / gath[pre, at, :]

    over_chunks(invert)
    gather_relay(0)
    gather_finish(0)
    (theta,) = dots(lambda at: (vec[at, :] * gath[0, at, :],), 1)

    def begin_residual(i, at):
        w = gath[0, at, :]
        img[at, :] = w
        r = (w - theta * vec[at, :]) * pinv[at, :]
        res[at, :] = r
        put_x(i, r)

    over_chunks(begin_residual)

    def early(at):
        v, w, r = vec[at, :], img[at, :], res[at, :]
        return v * v, v * w, v * r, r * r, r * w

    def rotate(theta, vv, vw, along, rr, rw, vh, rh):
        proj = rr - 2.0 * along * along + along * along * vv
        g = 1.0 / jnp.sqrt(proj + EPS)
        cross = 0.5 * g * ((vh - along * vw) + (rw - along * vw))
        diag_c = g * g * (rh - along * (rw + vh) + along * along * vw)
        half = 0.5 * (theta - diag_c)
        spread = jnp.sqrt(half * half + cross * cross)
        lowest = 0.5 * (theta + diag_c) - spread
        coef_x = spread - half
        coef_y = -cross
        length = jnp.sqrt(coef_x * coef_x + coef_y * coef_y)
        c_new = coef_y * g / length
        c_old = (coef_x - coef_y * g * along) / length
        return lowest, c_old, c_new

    def iterate(it, theta):
        multiply(it)
        known = dots(early, 5)
        gather_sent(it - 1)
        collect(it)
        gather_relay(it)
        gather_finish(it)

        def late(at):
            h = gath[it, at, :]
            return vec[at, :] * h, res[at, :] * h

        vh, rh = dots(late, 2)
        lowest, c_old, c_new = rotate(theta, *known, vh, rh)

        def update(i, at):
            v = c_old * vec[at, :] + c_new * res[at, :]
            w = c_old * img[at, :] + c_new * gath[it, at, :]
            vec[at, :] = v
            img[at, :] = w
            r = (w - lowest * v) * pinv[at, :]
            res[at, :] = r
            put_x(i, r)

        over_chunks(update)
        return lowest

    theta = lax.fori_loop(1, ITERS, iterate, theta)

    multiply(ITERS, last=True)
    me = me_s * terms + me_t

    def sc_copy(k):
        a, b = others[k]
        return pltpu.make_async_remote_copy(
            src_ref=scal.at[me], dst_ref=scal.at[me],
            send_sem=sc_send.at[0], recv_sem=sc_recv.at[me],
            device_id={"term": ring(me_t, b, terms), "sector": ring(me_s, a, sectors)},
            device_id_type=MESH,
        )

    vh, rh = jnp.zeros((8, width), F32), jnp.zeros((8, width), F32)
    for i in range(per_block):
        at = pl.ds(pl.multiple_of(me_s * width + i * CHUNK, CHUNK), CHUNK)
        h = part[ITERS, i * CHUNK : (i + 1) * CHUNK, :]
        vh = vh + fold(vec[at, :] * h)
        rh = rh + fold(res[at, :] * h)
    def narrow(value):
        value = value[0:4] + value[4:8]
        return sum(value[:, i * 128 : (i + 1) * 128] for i in range(width // 128))

    scal[me, 0:4, :] = narrow(vh)
    scal[me, 4:8, :] = narrow(rh)
    for k in range(len(others)):
        sc_copy(k).start()
    known = dots(early, 5)
    gather_sent(pre)
    gather_sent(ITERS - 1)
    for it in range(ITERS):
        for d in range(1, terms):
            rs_copy(it, d).wait_send()
    for a, b in others:
        source = ring(me_s, a, sectors) * terms + ring(me_t, b, terms)
        pltpu.make_async_remote_copy(
            src_ref=scal.at[source], dst_ref=scal.at[source],
            send_sem=sc_send.at[0], recv_sem=sc_recv.at[source],
            device_id={"sector": ring(me_s, 1, sectors)}, device_id_type=MESH,
        ).wait_recv()
    sums = jnp.sum(scal[...], axis=0)

    def whole_sum(value):
        value = jnp.sum(value, axis=0, keepdims=True)
        return jnp.sum(value, axis=1, keepdims=True) / count

    theta, c_old, c_new = rotate(theta, *known, whole_sum(sums[0:4]), whole_sum(sums[4:8]))
    ground_ref[...] = c_old * vec[own, :] + c_new * res[own, :]
    energy_ref[...] = jnp.broadcast_to(theta, energy_ref.shape)

    sent(scal.at[pl.ds(0, len(others))], sc_send.at[0])


def on_device(trial, precond, left_ops, right_ops, links, block_dims):
    sectors = lax.axis_size("sector")
    terms = lax.axis_size("term")
    _, rows, width = trial.shape
    own_terms = left_ops.shape[0]
    count = float(sectors * width * width)
    applies = ITERS + 1
    gathers = ITERS + 2
    whole = (sectors * width, width)
    vmem = pl.BlockSpec(memory_space=pltpu.VMEM)
    hbm = pl.BlockSpec(memory_space=pltpu.HBM)
    ground, energy = pl.pallas_call(
        functools.partial(kernel, sectors, terms, count),
        out_shape=(
            jax.ShapeDtypeStruct((rows, width), F32),
            jax.ShapeDtypeStruct((1, 128), F32),
        ),
        in_specs=[hbm] * 6,
        out_specs=(vmem, vmem),
        scratch_shapes=[
            pltpu.VMEM((gathers,) + whole, F32),
            pltpu.VMEM((applies, width, width), F32),
            pltpu.VMEM((ITERS, terms - 1, rows, width), F32),
            pltpu.VMEM(whole, F32),
            pltpu.VMEM(whole, F32),
            pltpu.VMEM(whole, F32),
            pltpu.VMEM(whole, F32),
            pltpu.VMEM((sectors + 1, 3 * width, width), BF16),
            pltpu.VMEM((own_terms, width, 3 * width), BF16),
            pltpu.VMEM((own_terms * 3 * width, width), BF16),
            pltpu.VMEM((width, own_terms * 3 * width), BF16),
            pltpu.VMEM((own_terms, width, width), F32),
            pltpu.VMEM((own_terms, width, width), F32),
            pltpu.VMEM((rows, width), F32),
            pltpu.VMEM((sectors * terms, 8, 128), F32),
            pltpu.SMEM((own_terms,), jnp.int32),
            pltpu.SMEM((2,), jnp.int32),
            pltpu.SemaphoreType.DMA((gathers,)),
            pltpu.SemaphoreType.DMA((gathers, sectors * terms * PARTS)),
            pltpu.SemaphoreType.DMA((ITERS, terms - 1)),
            pltpu.SemaphoreType.DMA((ITERS, terms - 1)),
            pltpu.SemaphoreType.DMA((1,)),
            pltpu.SemaphoreType.DMA((sectors * terms,)),
            pltpu.SemaphoreType.DMA((6,)),
        ],
        compiler_params=pltpu.CompilerParams(
            collective_id=0, has_side_effects=True, vmem_limit_bytes=60 * 2**20
        ),
    )(
        links.reshape(own_terms),
        block_dims.reshape(2),
        trial.reshape(rows, width),
        precond.reshape(rows, width),
        left_ops.reshape(own_terms, width, width),
        right_ops.reshape(own_terms, width, width),
    )
    return ground.reshape(1, rows, width), energy[0, :1]


def solution(mesh):
    in_specs = (
        P(("group", "sector"), "term", None),
        P(("group", "sector"), "term", None),
        P(("group", "term"), "sector", None, None),
        P(("group", "term"), "sector", None, None),
        P(("group", "term"), "sector"),
        P(("group", "sector"), None),
    )
    out_specs = (P(("group", "sector"), "term", None), P("group"))
    return jax.shard_map(
        on_device, mesh=mesh, in_specs=in_specs, out_specs=out_specs, check_vma=False
    )
```
